256 devices in a mesh: row: 16 (over z, y_hi), col: 16 (over y_lo, x, core).
Axes of the slice: x: 4, y: 4 (y_hi: 2, y_lo: 2; y = y_hi * 2 + y_lo), z: 8, core: 2. Of those that a mesh axis runs over, the one named last changes fastest.
Arguments:
- adjoint_in: bfloat16 [2, 16, 2560, 1536], P(None, None, 'col', 'row'), may hold values from -6 to 6
- solve_inverse: bfloat16 [16, 1536, 1536], P('row'), may hold values from -0.4 to 1.6
- gradient_fields: bfloat16 [4, 16, 1536, 3840], P(None, 'row', 'col'), may hold values from -5 to 5
Outputs:
- adjoint_out: float32 [2, 16, 2560, 1536], P(None, None, 'col', 'row')
The draws below stay inside these ranges and needn't reach their ends.
All inputs are finite; a program needn't handle non-finite values.
Results may differ from the reference program's by a relative error of at most 0.0032.
Values may be sent and summed in bfloat16 or wider, within the bound.
A program may use at most 64 MiB of HBM per device.

```python
import math
import jax
import jax.numpy as jnp
from jax import lax

NY = 1536
NZ = 3840
KZ = 2560
X = 16


def draw_solve_inverse(key, part):
    key = jax.random.fold_in(key, 11)
    first, second = jax.random.split(key, 2)
    offdiag = jnp.clip(jax.random.normal(first, (X, NY, NY), jnp.float32), -4.0, 4.0) * 0.5
    offdiag = offdiag / math.sqrt(NY)
    diagonal = jax.random.uniform(second, (X, NY), jnp.float32, 0.6, 1.2)
    identity = jnp.eye(NY, dtype=jnp.float32)
    return (offdiag + identity[None, :, :] * diagonal[:, :, None]).astype(jnp.bfloat16)


def block_scale(rng, extent, cuts, low, top_value):
    def one(axis_at, parts):
        steps = jax.random.uniform(jax.random.fold_in(jax.random.fold_in(rng, 6), axis_at), (parts,), jnp.float32, low / len(cuts), top_value / len(cuts))
        return jnp.repeat(jnp.exp(steps), extent[axis_at] // parts).reshape((-1,) + (1,) * (len(extent) - axis_at - 1))

    factor_of = one(*cuts[0])
    for cut in cuts[1:]:
        factor_of = factor_of * one(*cut)
    return factor_of


def noise(stream_key, extent, width, bound, cuts=(), held_as=jnp.bfloat16):
    factor_of = block_scale(stream_key, extent, cuts, -0.22, 0.18) if cuts else 1.0
    drawn = jax.random.normal(stream_key, extent, jnp.float32) * width * factor_of
    return jnp.minimum(jnp.maximum(drawn, -bound), bound).astype(held_as)


def setup_inputs(seed: int = 0) -> dict:
    key_list = jax.random.split(jax.random.key(seed), 4)
    adjoint_in = noise(key_list[0], (2, X, KZ, NY), 1.0, 6.0, ((2, 16), (3, 16)))
    solve_inverse = draw_solve_inverse(jax.random.fold_in(key_list[3], 71), 0)
    gradient_fields = noise(key_list[2], (4, X, NY, NZ), 0.7, 5.0, ((1, 16), (2, 16)))
    return dict(adjoint_in=adjoint_in, solve_inverse=solve_inverse, gradient_fields=gradient_fields)


step_weight = 0.5

def cheb_build(length_y):
    row_index = lax.broadcasted_iota(jnp.int32, (length_y, length_y), 0)
    col_index = lax.broadcasted_iota(jnp.int32, (length_y, length_y), 1)
    residue = row_index * col_index % (2 * (length_y - 1))
    angles = residue.astype(jnp.float32) * jnp.float32(math.pi / (length_y - 1))
    return (jnp.cos(angles) * jnp.float32(math.sqrt(2.0 / length_y))).astype(jnp.bfloat16)

def fourier_build(modes, points_z):
    mode_index = lax.broadcasted_iota(jnp.int32, (modes, points_z), 0)
    point_index = lax.broadcasted_iota(jnp.int32, (modes, points_z), 1)
    wavenumber = (mode_index + 1) // 2
    residue = wavenumber * point_index % points_z
    angles = residue.astype(jnp.float32) * jnp.float32(2.0 * math.pi / points_z)
    angles = angles - (mode_index % 2).astype(jnp.float32) * jnp.float32(math.pi / 2.0)
    return (jnp.cos(angles) * jnp.float32(math.sqrt(2.0 / points_z))).astype(jnp.bfloat16)

def reference(adjoint_in, solve_inverse, gradient_fields):
    cheb_table = cheb_build(NY)
    fourier = fourier_build(KZ, NZ)

    def one_plane(operands):
        adjoint, inverse, gradient = operands
        solved = jnp.dot(adjoint.reshape(2 * KZ, NY), inverse, preferred_element_type=jnp.float32)
        points = jnp.dot(solved.astype(jnp.bfloat16), cheb_table, preferred_element_type=jnp.float32).astype(jnp.bfloat16)
        points = points.reshape(2, KZ, NY).transpose(0, 2, 1).reshape(2 * NY, KZ)
        physical = jnp.dot(points, fourier, preferred_element_type=jnp.float32).reshape(2, NY, NZ)
        grads = gradient.astype(jnp.float32)
        force_u = grads[0] * physical[0] + grads[2] * physical[1]
        force_v = grads[1] * physical[0] + grads[3] * physical[1]
        forcing = jnp.stack([force_u, force_v]).astype(jnp.bfloat16).reshape(2 * NY, NZ)
        analysed = jnp.dot(forcing, fourier.T, preferred_element_type=jnp.float32).astype(jnp.bfloat16)
        analysed = analysed.reshape(2, NY, KZ).transpose(0, 2, 1).reshape(2 * KZ, NY)
        correction = jnp.dot(analysed, cheb_table, preferred_element_type=jnp.float32)
        return (solved + jnp.float32(step_weight) * correction).reshape(2, KZ, NY)
    result = lax.map(one_plane, (jnp.moveaxis(adjoint_in, 1, 0), solve_inverse, jnp.moveaxis(gradient_fields, 1, 0)))
    return jnp.moveaxis(result, 0, 1)
```

```python
import math

import jax
import jax.numpy as jnp
import ml_dtypes
import numpy as np
from jax import lax
from jax.sharding import PartitionSpec as P

NY = 1536
NZ = 3840
KZ = 2560


step_weight = 0.5


def cheb_build(length_y):
    index = np.arange(length_y, dtype=np.int64)
    residue = index[:, None] * index[None, :] % (2 * (length_y - 1))
    table = np.cos(np.arange(2 * (length_y - 1)) * (math.pi / (length_y - 1))) * math.sqrt(2.0 / length_y)
    return table.astype(np.float32).astype(ml_dtypes.bfloat16)[residue]


def fourier_build(modes, points_z):
    k = np.arange(modes, dtype=np.int64)
    residue = ((k + 1) // 2)[:, None] * np.arange(points_z, dtype=np.int64)[None, :] % points_z
    angles = np.arange(points_z) * (2.0 * math.pi / points_z)
    scale = math.sqrt(2.0 / points_z)
    both = np.stack([np.cos(angles), np.sin(angles)]) * scale
    both = both.astype(np.float32).astype(ml_dtypes.bfloat16)
    return both[(k % 2)[:, None], residue]


def on_device(adjoint_in, solve_inverse, gradient_fields):
    cheb_table = jnp.asarray(cheb_build(NY))
    fourier = jnp.asarray(fourier_build(KZ, NZ))
    gathered = lax.all_to_all(adjoint_in, "row", split_axis=1, concat_axis=3, tiled=True)
    solved = jnp.einsum(
        "cpkj,pji->cpki", gathered, solve_inverse, preferred_element_type=jnp.float32
    )
    points = jnp.einsum(
        "cpki,iy->cpky", solved.astype(jnp.bfloat16), cheb_table, preferred_element_type=jnp.float32
    ).astype(jnp.bfloat16)
    physical = jnp.einsum(
        "cpky,kz->cpyz",
        lax.all_to_all(points, "col", split_axis=3, concat_axis=2, tiled=True),
        fourier,
        preferred_element_type=jnp.float32,
    )
    grads = gradient_fields.astype(jnp.float32)
    force_u = grads[0] * physical[0] + grads[2] * physical[1]
    force_v = grads[1] * physical[0] + grads[3] * physical[1]
    forcing = jnp.stack([force_u, force_v]).astype(jnp.bfloat16)
    analysed = jnp.einsum(
        "cpyz,kz->cpky", forcing, fourier, preferred_element_type=jnp.float32
    ).astype(jnp.bfloat16)
    lines = lax.all_to_all(analysed, "col", split_axis=2, concat_axis=3, tiled=True)
    correction = jnp.einsum("cpky,yi->cpki", lines, cheb_table, preferred_element_type=jnp.float32)
    updated = solved + jnp.float32(step_weight) * correction
    sent = updated.astype(jnp.bfloat16)
    return lax.all_to_all(sent, "row", split_axis=3, concat_axis=1, tiled=True).astype(jnp.float32)


def solution(mesh):
    return jax.shard_map(
        on_device,
        mesh=mesh,
        in_specs=(P(None, None, "col", "row"), P("row", None, None), P(None, "row", "col", None)),
        out_specs=P(None, None, "col", "row"),
        check_vma=False,
    )
```

```python
import functools
import math

import jax
import jax.numpy as jnp
import ml_dtypes
import numpy as np
from jax import lax
from jax.experimental import pallas as pl
from jax.experimental.pallas import tpu as pltpu
from jax.sharding import PartitionSpec as P

NY = 1536
NZ = 3840
KZ = 2560

step_weight = 0.5

LANES = 128
SHARE = 96
CHUNKS = (32, 32, 32, 32, 32)
VMEM_LIMIT = 60 * 1024 * 1024
MESH = pl.DeviceIdType.MESH
NT = (((1,), (1,)), ((), ()))


def cheb_build(length_y):
    index = np.arange(length_y, dtype=np.int64)
    residue = index[:, None] * index[None, :] % (2 * (length_y - 1))
    table = np.cos(np.arange(2 * (length_y - 1)) * (math.pi / (length_y - 1))) * math.sqrt(2.0 / length_y)
    table = table.astype(np.float32).astype(ml_dtypes.bfloat16)[residue]
    table = table.reshape(length_y // SHARE, SHARE, length_y)
    table = np.pad(table, ((0, 0), (0, LANES - SHARE), (0, 0)))
    return table.reshape(-1, length_y)


def fourier_build(modes, points_z, devices, chunks):
    local = np.arange(modes, dtype=np.int64).reshape(devices, modes // devices)
    starts = np.cumsum((0,) + chunks)
    k = np.concatenate([local[:, a:b].reshape(-1) for a, b in zip(starts[:-1], starts[1:])])
    residue = ((k + 1) // 2)[:, None] * np.arange(points_z, dtype=np.int64)[None, :] % points_z
    angles = np.arange(points_z) * (2.0 * math.pi / points_z)
    both = np.stack([np.cos(angles), np.sin(angles)]) * math.sqrt(2.0 / points_z)
    both = both.astype(np.float32).astype(ml_dtypes.bfloat16)
    return both[(k % 2)[:, None], residue]


def lane_of(rows):
    return lax.broadcasted_iota(jnp.int32, (rows, LANES), 1)


def pack(first, second):
    rows = first.shape[0]
    half = rows // 2
    lane = lane_of(rows)
    turned = pltpu.roll(second, 96, 1)
    top = jnp.where(lane < 96, first, turned)
    low = jnp.where(lane[:half] < 64, turned[:half], pltpu.roll(turned[half:], 64, 1))
    return jnp.concatenate([top, low], axis=0).astype(jnp.bfloat16)


def unpack(block, rows):
    block = block.astype(jnp.float32)
    top, low = block[:rows], block[rows:]
    full = jnp.concatenate([low, pltpu.roll(low, 64, 1)], axis=0)
    second = pltpu.roll(jnp.where(lane_of(rows) < 64, full, top), 32, 1)
    return top, second


def kernel(
    chunks, adj, inv, grads, cheb, four, out,
    adj_v, inv_v, grads_v, cheb_v, four_v,
    send_a, recv_a, send_b, recv_b, send_c, recv_c, send_d, recv_d,
    lhs, solved, rounded, line, turned, phys, force, out_v,
    load_sem, send_sem, recv_sem, out_sem,
):
    f32, bf16 = jnp.float32, jnp.bfloat16
    groups = adj.shape[1]
    length_y = inv.shape[1]
    points_z = four.shape[1]
    row, col = lax.axis_index("row"), lax.axis_index("col")
    starts = [sum(chunks[:q]) for q in range(len(chunks))]
    count = len(chunks)
    tile = 256 if length_y % 256 == 0 else 128

    def local(source, target, sem):
        copy = pltpu.make_async_copy(source, target, sem)
        copy.start()
        return copy

    adj_loads = [
        local(adj.at[:, :, pl.ds(starts[q], chunks[q])], adj_v.at[:, :, pl.ds(starts[q], chunks[q])], load_sem.at[q])
        for q in range(count)
    ]
    for s in range(groups):
        local(inv.at[0, pl.ds(s * SHARE, SHARE)], inv_v.at[pl.ds(s * LANES, SHARE)], load_sem.at[count])
    cheb_load = local(cheb, cheb_v, load_sem.at[count + 1])
    four_loads = []
    for q in range(count):
        part = pl.ds(groups * starts[q], groups * chunks[q])
        four_loads.append(local(four.at[part], four_v.at[part], load_sem.at[count + 3 + q]))
    grads_load = local(grads, grads_v, load_sem.at[count + 2])

    barrier = pltpu.get_barrier_semaphore()

    def greet(t, carry):
        pl.semaphore_signal(barrier, inc=1, device_id={"row": lax.rem(row + t, groups)}, device_id_type=MESH)
        pl.semaphore_signal(barrier, inc=1, device_id={"col": lax.rem(col + t, groups)}, device_id_type=MESH)
        return carry

    lax.fori_loop(1, groups, greet, 0)

    def packed(q):
        return pl.ds(starts[q] * 3 // 2, chunks[q] * 3 // 2)

    def exchange_one(axis, phase, q, t, send, recv):
        me = row if axis == "row" else col
        peer = lax.rem(me + t, groups)
        pltpu.make_async_remote_copy(
            src_ref=send.at[peer, packed(q)],
            dst_ref=recv.at[me, packed(q)],
            send_sem=send_sem.at[phase, q],
            recv_sem=recv_sem.at[phase, q],
            device_id={axis: peer},
            device_id_type=MESH,
        ).start()

    def exchange(axis, phase, q, send, recv):
        def one(t, carry):
            exchange_one(axis, phase, q, t, send, recv)
            return carry

        lax.fori_loop(1, groups, one, 0)
        me = row if axis == "row" else col
        recv[me, packed(q)] = send[me, packed(q)]

    def arrived(phase, q, recv):
        every = recv.at[pl.ds(0, groups - 1), packed(q)]
        pltpu.make_async_copy(every, every, recv_sem.at[phase, q]).wait()

    def sent(phase, q, send):
        every = send.at[pl.ds(0, groups - 1), packed(q)]
        pltpu.make_async_copy(every, every, send_sem.at[phase, q]).wait()

    for s in range(groups):
        inv_v[s * LANES + SHARE : (s + 1) * LANES, :] = jnp.zeros((LANES - SHARE, length_y), bf16)
    for c in range(2):
        force[c * LANES + SHARE : (c + 1) * LANES, :] = jnp.zeros((LANES - SHARE, points_z), bf16)

    for q in range(count):
        size, at = chunks[q], starts[q]
        adj_loads[q].wait()

        def spread(p, carry, size=size, at=at, q=q):
            blank = jnp.zeros((size, LANES - SHARE), f32)
            parts = [
                jnp.concatenate([adj_v[c, p, pl.ds(at, size), :].astype(f32), blank], axis=1) for c in range(2)
            ]
            send_a[p, packed(q)] = pack(*parts)
            return carry

        lax.fori_loop(0, groups, spread, 0)
        if q == 0:
            pl.semaphore_wait(barrier, 2 * (groups - 1))
        exchange("row", 0, q, send_a, recv_a)

    def gather(q, recv):
        size = chunks[q]

        def one(s, carry):
            first, second = unpack(recv[s, packed(q)], size)
            at = pl.ds(pl.multiple_of(s * LANES, LANES), LANES)
            lhs[0:size, at] = first.astype(bf16)
            lhs[size : 2 * size, at] = second.astype(bf16)
            return carry

        lax.fori_loop(0, groups, one, 0)

    def to_points(q):
        size, at = chunks[q], starts[q]
        arrived(0, q, recv_a)
        gather(q, recv_a)
        if q == 0:
            whole = inv_v.at[pl.ds(0, groups * SHARE)]
            pltpu.make_async_copy(whole, whole, load_sem.at[count]).wait()

        def solve(n, carry):
            cols = pl.ds(pl.multiple_of(n * tile, tile), tile)
            value = jnp.dot(lhs[0 : 2 * size, :], inv_v[:, cols], preferred_element_type=f32)
            solved[2 * at : 2 * (at + size), cols] = value
            rounded[0 : 2 * size, cols] = value.astype(bf16)
            return carry

        lax.fori_loop(0, length_y // tile, solve, 0)
        if q == 0:
            cheb_load.wait()

        def evaluate(n, carry):
            rows = pl.ds(pl.multiple_of(n * 256, 256), 256)
            value = lax.dot_general(rounded[0 : 2 * size, :], cheb_v[rows, :], NT, preferred_element_type=f32)
            for j in range(2):
                part = slice(j * LANES, (j + 1) * LANES)
                send_b[2 * n + j, packed(q)] = pack(value[:size, part], value[size:, part])
            return carry

        lax.fori_loop(0, groups // 2, evaluate, 0)
        exchange("col", 1, q, send_b, recv_b)

    def to_physical(q):
        size, at = chunks[q], starts[q]
        depth = groups * size
        arrived(1, q, recv_b)

        def one(s, carry):
            first, second = unpack(recv_b[s, packed(q)], size)
            rows = pl.ds(pl.multiple_of(s * size, size), size)
            line[0, rows, :] = first
            line[1, rows, :] = second
            return carry

        lax.fori_loop(0, groups, one, 0)

        def turn(b, carry):
            rows = pl.ds(pl.multiple_of(b * LANES, LANES), LANES)
            for c in range(2):
                turned[c * LANES : (c + 1) * LANES, rows] = line[c, rows, :].T.astype(bf16)
            return carry

        lax.fori_loop(0, depth // LANES, turn, 0)
        four_loads[q].wait()
        if q == count - 1:
            grads_load.wait()

        def synthesise(n, carry):
            cols = pl.ds(pl.multiple_of(n * 256, 256), 256)
            value = jnp.dot(
                turned[:, 0:depth], four_v[groups * at : groups * (at + size), cols], preferred_element_type=f32
            )
            if q > 0:
                value = value + phys[:, cols]
            if q < count - 1:
                phys[:, cols] = value
            else:
                first, second = value[0:SHARE], value[LANES : LANES + SHARE]
                g = [grads_v[i, 0, :, cols].astype(f32) for i in range(4)]
                force[0:SHARE, cols] = (g[0] * first + g[2] * second).astype(bf16)
                force[LANES : LANES + SHARE, cols] = (g[1] * first + g[3] * second).astype(bf16)
            return carry

        lax.fori_loop(0, points_z // 256, synthesise, 0)

    def analyse(q):
        size, at = chunks[q], starts[q]
        several = max(1, min(groups, 256 // size))

        def one(n, carry):
            rows = pl.ds(pl.multiple_of(groups * at + n * (several * size), 16), several * size)
            value = lax.dot_general(four_v[rows, :], force[...], NT, preferred_element_type=f32)
            for j in range(several):
                part = value[j * size : (j + 1) * size]
                send_c[n * several + j, packed(q)] = pack(part[:, :LANES], part[:, LANES:])
            return carry

        lax.fori_loop(0, groups // several, one, 0)
        exchange("col", 2, q, send_c, recv_c)

    def update(q):
        size, at = chunks[q], starts[q]
        arrived(2, q, recv_c)
        gather(q, recv_c)

        def one(n, carry):
            cols = pl.ds(pl.multiple_of(n * 384, 384), 384)
            value = jnp.dot(lhs[0 : 2 * size, :], cheb_v[:, cols], preferred_element_type=f32)
            value = solved[2 * at : 2 * (at + size), cols] + f32(step_weight) * value
            lane = lane_of(size)
            shares = []
            for c in range(2):
                t = [value[c * size : (c + 1) * size, i * LANES : (i + 1) * LANES] for i in range(3)]
                shares.append([
                    t[0],
                    jnp.where(lane < 32, pltpu.roll(t[0], 32, 1), pltpu.roll(t[1], 32, 1)),
                    jnp.where(lane < 64, pltpu.roll(t[1], 64, 1), pltpu.roll(t[2], 64, 1)),
                    pltpu.roll(t[2], 96, 1),
                ])
            for j in range(4):
                send_d[4 * n + j, packed(q)] = pack(shares[0][j], shares[1][j])
            return carry

        lax.fori_loop(0, groups // 4, one, 0)
        exchange("row", 3, q, send_d, recv_d)

    def finish(q):
        size, at = chunks[q], starts[q]
        arrived(3, q, recv_d)

        def one(s, carry):
            for c, part in enumerate(unpack(recv_d[s, packed(q)], size)):
                out_v[c, s, pl.ds(at, size), :] = part[:, :SHARE].astype(bf16)
            return carry

        lax.fori_loop(0, groups, one, 0)
        return local(out_v.at[:, :, pl.ds(at, size)], out.at[:, :, pl.ds(at, size)], out_sem.at[q])

    for q in range(count):
        to_points(q)
        if q > 0:
            to_physical(q - 1)
    to_physical(count - 1)
    for q in range(count):
        analyse(q)
    for q in range(count):
        update(q)
    writes = [finish(q) for q in range(count)]
    for q in range(count):
        for phase, send in enumerate((send_a, send_b, send_c, send_d)):
            sent(phase, q, send)
        writes[q].wait()


def on_device(groups, chunks, adjoint_in, solve_inverse, gradient_fields):
    local_modes = adjoint_in.shape[2]
    length_y = solve_inverse.shape[1]
    points_z = gradient_fields.shape[3]
    cheb = jnp.asarray(cheb_build(length_y))
    four = jnp.asarray(fourier_build(local_modes * groups, points_z, groups, chunks))
    f32, bf16 = jnp.float32, jnp.bfloat16
    most = max(chunks)
    count = len(chunks)
    mail = pltpu.VMEM((groups, local_modes * 3 // 2, LANES), bf16)
    result = pl.pallas_call(
        functools.partial(kernel, chunks),
        out_shape=jax.ShapeDtypeStruct(adjoint_in.shape, bf16),
        in_specs=[pl.BlockSpec(memory_space=pl.ANY)] * 5,
        out_specs=pl.BlockSpec(memory_space=pl.ANY),
        scratch_shapes=[
            pltpu.VMEM(adjoint_in.shape, bf16),
            pltpu.VMEM(cheb.shape, bf16),
            pltpu.VMEM(gradient_fields.shape, bf16),
            pltpu.VMEM(cheb.shape, bf16),
            pltpu.VMEM(four.shape, bf16),
            *[mail] * 8,
            pltpu.VMEM((2 * most, groups * LANES), bf16),
            pltpu.VMEM((2 * local_modes, length_y), f32),
            pltpu.VMEM((2 * most, length_y), bf16),
            pltpu.VMEM((2, groups * most, LANES), f32),
            pltpu.VMEM((2 * LANES, groups * most), bf16),
            pltpu.VMEM((2 * LANES, points_z), f32),
            pltpu.VMEM((2 * LANES, points_z), bf16),
            pltpu.VMEM(adjoint_in.shape, bf16),
            pltpu.SemaphoreType.DMA((2 * count + 3,)),
            pltpu.SemaphoreType.DMA((4, count)),
            pltpu.SemaphoreType.DMA((4, count)),
            pltpu.SemaphoreType.DMA((count,)),
        ],
        compiler_params=pltpu.CompilerParams(
            collective_id=0, has_side_effects=True, vmem_limit_bytes=VMEM_LIMIT
        ),
        cost_estimate=pl.CostEstimate(flops=12_000_000_000, bytes_accessed=40_000_000, transcendentals=0),
    )(adjoint_in, solve_inverse, gradient_fields, cheb, four)
    return result.astype(f32)


def solution(mesh):
    groups = mesh.shape["row"]
    return jax.shard_map(
        functools.partial(on_device, groups, CHUNKS),
        mesh=mesh,
        in_specs=(P(None, None, "col", "row"), P("row", None, None), P(None, "row", "col", None)),
        out_specs=P(None, None, "col", "row"),
        check_vma=False,
    )
```

```python
import functools
import math

import jax
import jax.numpy as jnp
import ml_dtypes
import numpy as np
from jax import lax
from jax.experimental import pallas as pl
from jax.experimental.pallas import tpu as pltpu
from jax.sharding import PartitionSpec as P

NY = 1536
NZ = 3840
KZ = 2560

step_weight = 0.5

LANES = 128
BLOCK = 256
BATCH = 16
SHARE = 96
CHUNKS = (64, 64, 32)
SOLVE_TILE = 768
POST = 4
WIDTH = 640
VMEM_LIMIT = 60 * 1024 * 1024
MESH = pl.DeviceIdType.MESH
NT = (((1,), (1,)), ((), ()))


def cheb_build(length_y):
    index = np.arange(length_y, dtype=np.int64)
    residue = index[:, None] * index[None, :] % (2 * (length_y - 1))
    table = np.cos(np.arange(2 * (length_y - 1)) * (math.pi / (length_y - 1))) * math.sqrt(2.0 / length_y)
    return table.astype(np.float32).astype(ml_dtypes.bfloat16)[residue]


def parity_order():
    n = np.arange(BLOCK)
    odd = (n + 1) // 2 % 2
    return np.concatenate([n[odd == 0], n[odd == 1]])


def parity_build():
    forward = np.zeros((BLOCK, BLOCK), np.float32)
    forward[parity_order(), np.arange(BLOCK)] = 1.0
    return forward.astype(ml_dtypes.bfloat16)


def fourier_build(modes, points_z, devices, chunks):
    local = np.arange(modes, dtype=np.int64).reshape(devices, modes // devices)
    starts = np.cumsum((0,) + chunks)
    k = np.concatenate([local[:, a:b].reshape(-1) for a, b in zip(starts[:-1], starts[1:])])
    k = k.reshape(-1, BLOCK)[:, parity_order()].reshape(-1, 2, BLOCK // 2)
    k = k.transpose(1, 0, 2).reshape(2, modes // 2, 1)
    residue = (k + 1) // 2 * np.arange(points_z // 2, dtype=np.int64) % points_z
    angles = np.arange(points_z) * (2.0 * math.pi / points_z)
    both = np.stack([np.cos(angles), np.sin(angles)]) * math.sqrt(2.0 / points_z)
    both = both.astype(np.float32).astype(ml_dtypes.bfloat16)
    return both[k % 2, residue]


def below(shape, limit):
    return lax.broadcasted_iota(jnp.int16, shape, len(shape) - 1) < jnp.int16(limit)


def pack(first, second):
    half, last = first.shape[-2] // 2, first.ndim - 1
    turned = pltpu.roll(second, 96, last)
    top = jnp.where(below(first.shape, 96), first, turned)
    upper, lower = turned[..., :half, :], turned[..., half:, :]
    low = jnp.where(below(upper.shape, 64), upper, pltpu.roll(lower, 64, last))
    return jnp.concatenate([top, low], axis=last - 1)


def unpack(block):
    rows, last = block.shape[-2] * 2 // 3, block.ndim - 1
    top, low = block[..., :rows, :], block[..., rows:, :]
    full = jnp.concatenate([low, pltpu.roll(low, 64, last)], axis=last - 1)
    second = pltpu.roll(jnp.where(below(top.shape, 64), full, top), 32, last)
    return top, second


def spread_lanes(tiles):
    shape = tiles[0].shape
    middle = [pltpu.roll(t, 32, 1) for t in tiles[:2]], [pltpu.roll(t, 64, 1) for t in tiles[1:]]
    return [
        tiles[0],
        jnp.where(below(shape, 32), *middle[0]),
        jnp.where(below(shape, 64), *middle[1]),
        pltpu.roll(tiles[2], 96, 1),
    ]


def close_lanes(parts):
    shape = parts[0].shape
    turned = [pltpu.roll(p, shift, 1) for p, shift in zip(parts[1:], (96, 64, 32))]
    return [
        jnp.where(below(shape, 96), parts[0], turned[0]),
        jnp.where(below(shape, 64), turned[0], turned[1]),
        jnp.where(below(shape, 32), turned[1], turned[2]),
    ]


def kernel(
    chunks, adj, inv, grads, cheb, four, parity, out,
    adj_v, inv_v, grads_v, cheb_v, four_v, parity_v,
    send_a, recv_a, send_b, recv_b, send_c, recv_c, send_d, recv_d,
    lhs, solved, rounded, turned, sorted_v, phys, force, out_v,
    load_sem, send_sem, recv_sem, out_sem,
):
    f32, bf16 = jnp.float32, jnp.bfloat16
    groups = adj.shape[1]
    length_y = inv.shape[1]
    half_z = four.shape[2]
    row, col = lax.axis_index("row"), lax.axis_index("col")
    starts = [sum(chunks[:q]) for q in range(len(chunks))]
    count = len(chunks)
    tile = math.gcd(length_y, SOLVE_TILE)
    quads = min(POST, groups // 4)

    def local(source, target, sem):
        copy = pltpu.make_async_copy(source, target, sem)
        copy.start()
        return copy

    adj_loads = [
        local(adj.at[:, :, pl.ds(starts[q], chunks[q])], adj_v.at[:, :, pl.ds(starts[q], chunks[q])], load_sem.at[q])
        for q in range(count)
    ]
    barrier = pltpu.get_barrier_semaphore()

    def greet(t, carry):
        pl.semaphore_signal(barrier, inc=1, device_id={"row": lax.rem(row + t, groups)}, device_id_type=MESH)
        pl.semaphore_signal(barrier, inc=1, device_id={"col": lax.rem(col + t, groups)}, device_id_type=MESH)
        return carry

    lax.fori_loop(1, groups, greet, 0)
    inv_load = local(inv.at[0], inv_v, load_sem.at[count])
    cheb_load = local(cheb, cheb_v, load_sem.at[count + 1])
    parity_load = local(parity, parity_v, load_sem.at[count + 3])
    four_loads = []
    for q in range(count):
        part = pl.ds(groups * starts[q] // 2, groups * chunks[q] // 2)
        four_loads.append(local(four.at[:, part], four_v.at[:, part], load_sem.at[count + 4 + q]))
    grads_load = local(grads, grads_v, load_sem.at[count + 2])

    def packed(q):
        return pl.ds(starts[q] * 3 // 2, chunks[q] * 3 // 2)

    def exchange_one(axis, phase, q, t, send, recv):
        me = row if axis == "row" else col
        peer = lax.rem(me + t, groups)
        pltpu.make_async_remote_copy(
            src_ref=send.at[peer, packed(q)],
            dst_ref=recv.at[me, packed(q)],
            send_sem=send_sem.at[phase, q],
            recv_sem=recv_sem.at[phase, q],
            device_id={axis: peer},
            device_id_type=MESH,
        ).start()

    def exchange(axis, phase, q, send, recv):
        def one(t, carry):
            exchange_one(axis, phase, q, t, send, recv)
            return carry

        lax.fori_loop(1, groups, one, 0)
        me = row if axis == "row" else col
        recv[me, packed(q)] = send[me, packed(q)]

    def arrived(phase, q, recv):
        every = recv.at[pl.ds(0, groups - 1), packed(q)]
        pltpu.make_async_copy(every, every, recv_sem.at[phase, q]).wait()

    def sent(phase, q, send):
        every = send.at[pl.ds(0, groups - 1), packed(q)]
        pltpu.make_async_copy(every, every, send_sem.at[phase, q]).wait()

    for half in range(2):
        for c in range(2):
            force[half, c * LANES + SHARE : (c + 1) * LANES, :] = jnp.zeros((LANES - SHARE, half_z), bf16)

    for q in range(count):
        size, at = chunks[q], starts[q]
        adj_loads[q].wait()

        def spread(p, carry, size=size, at=at, q=q):
            blank = jnp.zeros((BATCH, size, LANES - SHARE), bf16)
            some = pl.ds(p * BATCH, BATCH)
            parts = [jnp.concatenate([adj_v[c, some, pl.ds(at, size), :], blank], axis=2) for c in range(2)]
            send_a[some, packed(q)] = pack(*parts)
            return carry

        lax.fori_loop(0, groups // BATCH, spread, 0)
        if q == 0:
            pl.semaphore_wait(barrier, 2 * (groups - 1))
        exchange("row", 0, q, send_a, recv_a)

    def gather(q, recv):
        size = chunks[q]

        def one(s, carry):
            first, second = unpack(recv[pl.ds(s * BATCH, BATCH), packed(q)])
            for c, parts in enumerate((first, second)):
                for quad in range(BATCH // 4):
                    for i, tile in enumerate(close_lanes([parts[4 * quad + i] for i in range(4)])):
                        at = pl.ds(pl.multiple_of(s * (BATCH * SHARE), LANES) + (3 * quad + i) * LANES, LANES)
                        lhs[c * size : (c + 1) * size, at] = tile
            return carry

        lax.fori_loop(0, groups // BATCH, one, 0)

    def post(n, q, value, send):
        size = chunks[q]
        for quad in range(quads):
            tiles = [slice((3 * quad + i) * LANES, (3 * quad + i + 1) * LANES) for i in range(3)]
            first, second = (
                spread_lanes([value[c * size : (c + 1) * size, tile] for tile in tiles]) for c in range(2)
            )
            for j in range(4):
                send[4 * (quads * n + quad) + j, packed(q)] = pack(first[j], second[j])

    def to_points(q):
        size, at = chunks[q], starts[q]
        arrived(0, q, recv_a)
        gather(q, recv_a)
        if q == 0:
            inv_load.wait()

        def solve(n, carry):
            cols = pl.ds(pl.multiple_of(n * tile, tile), tile)
            value = jnp.dot(lhs[0 : 2 * size, :], inv_v[:, cols], preferred_element_type=f32)
            solved[2 * at : 2 * (at + size), cols] = value
            rounded[0 : 2 * size, cols] = value.astype(bf16)
            return carry

        lax.fori_loop(0, length_y // tile, solve, 0)
        if q == 0:
            cheb_load.wait()

        def evaluate(n, carry):
            cols = pl.ds(pl.multiple_of(n * (384 * quads), 384), 384 * quads)
            value = jnp.dot(rounded[0 : 2 * size, :], cheb_v[:, cols], preferred_element_type=f32)
            post(n, q, value.astype(bf16), send_b)
            return carry

        lax.fori_loop(0, groups // (4 * quads), evaluate, 0)
        exchange("col", 1, q, send_b, recv_b)

    def to_physical(q):
        size, at = chunks[q], starts[q]
        depth = groups * size
        arrived(1, q, recv_b)

        def one(s, carry):
            rows = pl.ds(pl.multiple_of(s * (BATCH * size), LANES), BATCH * size)
            for c, part in enumerate(unpack(recv_b[pl.ds(s * BATCH, BATCH), packed(q)])):
                turned[c * LANES : (c + 1) * LANES, rows] = part.reshape(BATCH * size, LANES).T
            return carry

        lax.fori_loop(0, groups // BATCH, one, 0)
        if q == 0:
            parity_load.wait()

        def sort(b, carry):
            cols = pl.ds(pl.multiple_of(b * BLOCK, BLOCK), BLOCK)
            value = jnp.dot(turned[:, cols], parity_v[...], preferred_element_type=f32).astype(bf16)
            half = pl.ds(pl.multiple_of(b * LANES, LANES), LANES)
            for parity in range(2):
                sorted_v[parity, :, half] = value[:, parity * LANES : (parity + 1) * LANES]
            return carry

        lax.fori_loop(0, depth // BLOCK, sort, 0)
        four_loads[q].wait()
        if q == count - 1:
            grads_load.wait()

        def synthesise(start, width):
            cols = pl.ds(start, width)
            rows = slice(groups * at // 2, groups * (at + size) // 2)
            values = []
            for parity in range(2):
                value = jnp.dot(
                    sorted_v[parity, :, 0 : depth // 2], four_v[parity, rows, cols], preferred_element_type=f32
                )
                values.append(value if q == 0 else value + phys[parity, :, cols])
            if q < count - 1:
                for parity in range(2):
                    phys[parity, :, cols] = values[parity]
                return
            forces = []
            for half in range(2):
                value = values[0] + values[1] if half == 0 else values[0] - values[1]
                first, second = value[0:SHARE], value[LANES : LANES + SHARE]
                g = [grads_v[i, 0, :, pl.ds(start + half * half_z, width)].astype(f32) for i in range(4)]
                forces.append((g[0] * first + g[2] * second, g[1] * first + g[3] * second))
            for c in range(2):
                rows = slice(c * LANES, c * LANES + SHARE)
                force[0, rows, cols] = (forces[0][c] + forces[1][c]).astype(bf16)
                force[1, rows, cols] = (forces[0][c] - forces[1][c]).astype(bf16)

        def synthesise_one(n, carry):
            synthesise(pl.multiple_of(n * WIDTH, LANES), WIDTH)
            return carry

        lax.fori_loop(0, half_z // WIDTH, synthesise_one, 0)
        if half_z % WIDTH:
            synthesise(half_z // WIDTH * WIDTH, half_z % WIDTH)

    def analyse(q):
        size, at = chunks[q], starts[q]
        several = BLOCK // size

        def one(n, carry):
            rows = pl.ds(pl.multiple_of(groups * at // 2 + n * BLOCK, BLOCK), BLOCK)
            halves = [
                lax.dot_general(four_v[parity, rows, :], force[parity], NT, preferred_element_type=f32).astype(bf16)
                for parity in range(2)
            ]
            for b in range(2):
                part = slice(b * LANES, (b + 1) * LANES)
                value = jnp.concatenate([halves[0][part], halves[1][part]], axis=0)
                value = jnp.dot(parity_v[...], value, preferred_element_type=f32).astype(bf16)
                for j in range(several):
                    block = value[j * size : (j + 1) * size]
                    letter = pack(block[:, :LANES], block[:, LANES:])
                    send_c[(2 * n + b) * several + j, packed(q)] = letter
            return carry

        lax.fori_loop(0, groups // (2 * several), one, 0)
        exchange("col", 2, q, send_c, recv_c)

    def update(q):
        size, at = chunks[q], starts[q]
        arrived(2, q, recv_c)
        gather(q, recv_c)

        def one(n, carry):
            cols = pl.ds(pl.multiple_of(n * (384 * quads), 384), 384 * quads)
            value = jnp.dot(lhs[0 : 2 * size, :], cheb_v[:, cols], preferred_element_type=f32)
            value = solved[2 * at : 2 * (at + size), cols] + f32(step_weight) * value
            post(n, q, value.astype(bf16), send_d)
            return carry

        lax.fori_loop(0, groups // (4 * quads), one, 0)
        exchange("row", 3, q, send_d, recv_d)

    def finish(q):
        size, at = chunks[q], starts[q]
        arrived(3, q, recv_d)

        def one(s, carry):
            some = pl.ds(s * BATCH, BATCH)
            for c, part in enumerate(unpack(recv_d[some, packed(q)])):
                out_v[c, some, pl.ds(at, size), :] = part[..., :SHARE]
            return carry

        lax.fori_loop(0, groups // BATCH, one, 0)
        return local(out_v.at[:, :, pl.ds(at, size)], out.at[:, :, pl.ds(at, size)], out_sem.at[q])

    for q in range(count):
        to_points(q)
        if 0 < q < count - 1:
            to_physical(q - 1)
    to_physical(count - 2)
    to_physical(count - 1)
    order = list(reversed(range(count)))
    analyse(order[0])
    for q, ahead in zip(order, order[1:] + [None]):
        if ahead is not None:
            analyse(ahead)
        update(q)
    writes = [finish(q) for q in order]
    for q in range(count):
        for phase, send in enumerate((send_a, send_b, send_c, send_d)):
            sent(phase, q, send)
        writes[q].wait()


def on_device(groups, chunks, adjoint_in, solve_inverse, gradient_fields):
    local_modes = adjoint_in.shape[2]
    length_y = solve_inverse.shape[1]
    points_z = gradient_fields.shape[3]
    cheb = jnp.asarray(cheb_build(length_y))
    parity = jnp.asarray(parity_build())
    four = jnp.asarray(fourier_build(local_modes * groups, points_z, groups, chunks))
    f32, bf16 = jnp.float32, jnp.bfloat16
    most = max(chunks)
    count = len(chunks)
    mail = pltpu.VMEM((groups, local_modes * 3 // 2, LANES), bf16)
    result = pl.pallas_call(
        functools.partial(kernel, chunks),
        out_shape=jax.ShapeDtypeStruct(adjoint_in.shape, bf16),
        in_specs=[pl.BlockSpec(memory_space=pl.ANY)] * 6,
        out_specs=pl.BlockSpec(memory_space=pl.ANY),
        scratch_shapes=[
            pltpu.VMEM(adjoint_in.shape, bf16),
            pltpu.VMEM(solve_inverse.shape[1:], bf16),
            pltpu.VMEM(gradient_fields.shape, bf16),
            pltpu.VMEM(cheb.shape, bf16),
            pltpu.VMEM(four.shape, bf16),
            pltpu.VMEM(parity.shape, bf16),
            *[mail] * 8,
            pltpu.VMEM((2 * most, length_y), bf16),
            pltpu.VMEM((2 * local_modes, length_y), f32),
            pltpu.VMEM((2 * most, length_y), bf16),
            pltpu.VMEM((2 * LANES, groups * most), bf16),
            pltpu.VMEM((2, 2 * LANES, groups * most // 2), bf16),
            pltpu.VMEM((2, 2 * LANES, points_z // 2), f32),
            pltpu.VMEM((2, 2 * LANES, points_z // 2), bf16),
            pltpu.VMEM(adjoint_in.shape, bf16),
            pltpu.SemaphoreType.DMA((2 * count + 4,)),
            pltpu.SemaphoreType.DMA((4, count)),
            pltpu.SemaphoreType.DMA((4, count)),
            pltpu.SemaphoreType.DMA((count,)),
        ],
        compiler_params=pltpu.CompilerParams(
            collective_id=0, has_side_effects=True, vmem_limit_bytes=VMEM_LIMIT
        ),
        cost_estimate=pl.CostEstimate(flops=12_000_000_000, bytes_accessed=40_000_000, transcendentals=0),
    )(adjoint_in, solve_inverse, gradient_fields, cheb, four, parity)
    return result.astype(f32)


def solution(mesh):
    groups = mesh.shape["row"]
    return jax.shard_map(
        functools.partial(on_device, groups, CHUNKS),
        mesh=mesh,
        in_specs=(P(None, None, "col", "row"), P("row", None, None), P(None, "row", "col", None)),
        out_specs=P(None, None, "col", "row"),
        check_vma=False,
    )
```

```python
import functools
import math

import jax
import jax.numpy as jnp
import ml_dtypes
import numpy as np
from jax import lax
from jax.experimental import pallas as pl
from jax.experimental.pallas import tpu as pltpu
from jax.sharding import PartitionSpec as P

NY = 1536
NZ = 3840
KZ = 2560

step_weight = 0.5

LANES = 128
BLOCK = 256
BATCH = 16
SHARE = 96
CHUNKS = (64, 32, 32, 32)
SOLVE_TILE = 768
POST = 4
WIDTH = 640
VMEM_LIMIT = 60 * 1024 * 1024
MESH = pl.DeviceIdType.MESH
NT = (((1,), (1,)), ((), ()))


def cheb_build(length_y):
    index = np.arange(length_y, dtype=np.int64)
    residue = index[:, None] * index[None, :] % (2 * (length_y - 1))
    table = np.cos(np.arange(2 * (length_y - 1)) * (math.pi / (length_y - 1))) * math.sqrt(2.0 / length_y)
    return table.astype(np.float32).astype(ml_dtypes.bfloat16)[residue]


def parity_order():
    n = np.arange(BLOCK)
    odd = (n + 1) // 2 % 2
    return np.concatenate([n[odd == 0], n[odd == 1]])


def parity_build():
    forward = np.zeros((BLOCK, BLOCK), np.float32)
    forward[parity_order(), np.arange(BLOCK)] = 1.0
    return forward.astype(ml_dtypes.bfloat16)


def fourier_build(modes, points_z, devices, chunks):
    local = np.arange(modes, dtype=np.int64).reshape(devices, modes // devices)
    starts = np.cumsum((0,) + chunks)
    k = np.concatenate([local[:, a:b].reshape(-1) for a, b in zip(starts[:-1], starts[1:])])
    k = k.reshape(-1, BLOCK)[:, parity_order()].reshape(-1, 2, BLOCK // 2)
    k = k.transpose(1, 0, 2).reshape(2, modes // 2, 1)
    residue = (k + 1) // 2 * np.arange(points_z // 2, dtype=np.int64) % points_z
    angles = np.arange(points_z) * (2.0 * math.pi / points_z)
    both = np.stack([np.cos(angles), np.sin(angles)]) * math.sqrt(2.0 / points_z)
    both = both.astype(np.float32).astype(ml_dtypes.bfloat16)
    return both[k % 2, residue]


def below(shape, limit):
    return lax.broadcasted_iota(jnp.int16, shape, len(shape) - 1) < jnp.int16(limit)


def pack(first, second):
    half, last = first.shape[-2] // 2, first.ndim - 1
    turned = pltpu.roll(second, 96, last)
    top = jnp.where(below(first.shape, 96), first, turned)
    upper, lower = turned[..., :half, :], turned[..., half:, :]
    low = jnp.where(below(upper.shape, 64), upper, pltpu.roll(lower, 64, last))
    return jnp.concatenate([top, low], axis=last - 1)


def unpack(block):
    rows, last = block.shape[-2] * 2 // 3, block.ndim - 1
    top, low = block[..., :rows, :], block[..., rows:, :]
    full = jnp.concatenate([low, pltpu.roll(low, 64, last)], axis=last - 1)
    second = pltpu.roll(jnp.where(below(top.shape, 64), full, top), 32, last)
    return top, second


def spread_lanes(tiles):
    shape = tiles[0].shape
    middle = [pltpu.roll(t, 32, 1) for t in tiles[:2]], [pltpu.roll(t, 64, 1) for t in tiles[1:]]
    return [
        tiles[0],
        jnp.where(below(shape, 32), *middle[0]),
        jnp.where(below(shape, 64), *middle[1]),
        pltpu.roll(tiles[2], 96, 1),
    ]


def close_lanes(parts):
    shape = parts[0].shape
    turned = [pltpu.roll(p, shift, 1) for p, shift in zip(parts[1:], (96, 64, 32))]
    return [
        jnp.where(below(shape, 96), parts[0], turned[0]),
        jnp.where(below(shape, 64), turned[0], turned[1]),
        jnp.where(below(shape, 32), turned[1], turned[2]),
    ]


def kernel(
    chunks, adj, inv, grads, cheb, four, parity, out,
    adj_v, inv_v, grads_v, cheb_v, four_v, parity_v,
    send_a, recv_a, send_b, recv_b, send_c, recv_c, send_d, recv_d,
    lhs, solved, rounded, turned, sorted_v, phys, force, out_v,
    load_sem, send_sem, recv_sem, out_sem,
):
    f32, bf16 = jnp.float32, jnp.bfloat16
    groups = adj.shape[1]
    length_y = inv.shape[1]
    half_z = four.shape[2]
    row, col = lax.axis_index("row"), lax.axis_index("col")
    starts = [sum(chunks[:q]) for q in range(len(chunks))]
    count = len(chunks)
    tile = math.gcd(length_y, SOLVE_TILE)
    quads = min(POST, groups // 4)

    def local(source, target, sem):
        copy = pltpu.make_async_copy(source, target, sem)
        copy.start()
        return copy

    adj_loads = [
        local(adj.at[:, :, pl.ds(starts[q], chunks[q])], adj_v.at[:, :, pl.ds(starts[q], chunks[q])], load_sem.at[q])
        for q in range(count)
    ]
    barrier = pltpu.get_barrier_semaphore()

    def greet(t, carry):
        pl.semaphore_signal(barrier, inc=1, device_id={"row": lax.rem(row + t, groups)}, device_id_type=MESH)
        pl.semaphore_signal(barrier, inc=1, device_id={"col": lax.rem(col + t, groups)}, device_id_type=MESH)
        return carry

    lax.fori_loop(1, groups, greet, 0)
    inv_load = local(inv.at[0], inv_v, load_sem.at[count])
    cheb_load = local(cheb, cheb_v, load_sem.at[count + 1])
    parity_load = local(parity, parity_v, load_sem.at[count + 3])
    four_loads = []
    for q in range(count):
        part = pl.ds(groups * starts[q] // 2, groups * chunks[q] // 2)
        four_loads.append(local(four.at[:, part], four_v.at[:, part], load_sem.at[count + 4 + q]))
    grads_load = local(grads, grads_v, load_sem.at[count + 2])

    def packed(q):
        return pl.ds(starts[q] * 3 // 2, chunks[q] * 3 // 2)

    def exchange_one(axis, phase, q, t, send, recv):
        me = row if axis == "row" else col
        peer = lax.rem(me + t, groups)
        pltpu.make_async_remote_copy(
            src_ref=send.at[peer, packed(q)],
            dst_ref=recv.at[me, packed(q)],
            send_sem=send_sem.at[phase, q],
            recv_sem=recv_sem.at[phase, q],
            device_id={axis: peer},
            device_id_type=MESH,
        ).start()

    def exchange(axis, phase, q, send, recv):
        def one(t, carry):
            exchange_one(axis, phase, q, t, send, recv)
            return carry

        lax.fori_loop(1, groups, one, 0)
        me = row if axis == "row" else col
        recv[me, packed(q)] = send[me, packed(q)]

    def arrived(phase, q, recv):
        every = recv.at[pl.ds(0, groups - 1), packed(q)]
        pltpu.make_async_copy(every, every, recv_sem.at[phase, q]).wait()

    def sent(phase, q, send):
        every = send.at[pl.ds(0, groups - 1), packed(q)]
        pltpu.make_async_copy(every, every, send_sem.at[phase, q]).wait()

    for half in range(2):
        for c in range(2):
            force[half, c * LANES + SHARE : (c + 1) * LANES, :] = jnp.zeros((LANES - SHARE, half_z), bf16)

    for q in range(count):
        size, at = chunks[q], starts[q]
        adj_loads[q].wait()

        def spread(p, carry, size=size, at=at, q=q):
            blank = jnp.zeros((BATCH, size, LANES - SHARE), bf16)
            some = pl.ds(p * BATCH, BATCH)
            parts = [jnp.concatenate([adj_v[c, some, pl.ds(at, size), :], blank], axis=2) for c in range(2)]
            send_a[some, packed(q)] = pack(*parts)
            return carry

        lax.fori_loop(0, groups // BATCH, spread, 0)
        if q == 0:
            pl.semaphore_wait(barrier, 2 * (groups - 1))
        exchange("row", 0, q, send_a, recv_a)

    def gather(q, recv):
        size = chunks[q]

        def one(s, carry):
            first, second = unpack(recv[pl.ds(s * BATCH, BATCH), packed(q)])
            for c, parts in enumerate((first, second)):
                for quad in range(BATCH // 4):
                    for i, tile in enumerate(close_lanes([parts[4 * quad + i] for i in range(4)])):
                        at = pl.ds(pl.multiple_of(s * (BATCH * SHARE), LANES) + (3 * quad + i) * LANES, LANES)
                        lhs[c * size : (c + 1) * size, at] = tile
            return carry

        lax.fori_loop(0, groups // BATCH, one, 0)

    def post(n, q, value, send):
        size = chunks[q]
        for quad in range(quads):
            tiles = [slice((3 * quad + i) * LANES, (3 * quad + i + 1) * LANES) for i in range(3)]
            first, second = (
                spread_lanes([value[c * size : (c + 1) * size, tile] for tile in tiles]) for c in range(2)
            )
            for j in range(4):
                send[4 * (quads * n + quad) + j, packed(q)] = pack(first[j], second[j])

    def to_points(q):
        size, at = chunks[q], starts[q]
        arrived(0, q, recv_a)
        gather(q, recv_a)
        if q == 0:
            inv_load.wait()

        def solve(n, carry):
            cols = pl.ds(pl.multiple_of(n * tile, tile), tile)
            value = jnp.dot(lhs[0 : 2 * size, :], inv_v[:, cols], preferred_element_type=f32)
            solved[2 * at : 2 * (at + size), cols] = value
            rounded[0 : 2 * size, cols] = value.astype(bf16)
            return carry

        lax.fori_loop(0, length_y // tile, solve, 0)
        if q == 0:
            cheb_load.wait()

        def evaluate(n, carry):
            cols = pl.ds(pl.multiple_of(n * (384 * quads), 384), 384 * quads)
            value = jnp.dot(rounded[0 : 2 * size, :], cheb_v[:, cols], preferred_element_type=f32)
            post(n, q, value.astype(bf16), send_b)
            return carry

        lax.fori_loop(0, groups // (4 * quads), evaluate, 0)
        exchange("col", 1, q, send_b, recv_b)

    def to_physical(q):
        size, at = chunks[q], starts[q]
        depth = groups * size
        arrived(1, q, recv_b)

        def one(s, carry):
            rows = pl.ds(pl.multiple_of(s * (BATCH * size), LANES), BATCH * size)
            for c, part in enumerate(unpack(recv_b[pl.ds(s * BATCH, BATCH), packed(q)])):
                turned[c * LANES : (c + 1) * LANES, rows] = part.reshape(BATCH * size, LANES).T
            return carry

        lax.fori_loop(0, groups // BATCH, one, 0)
        if q == 0:
            parity_load.wait()

        def sort(b, carry):
            cols = pl.ds(pl.multiple_of(b * BLOCK, BLOCK), BLOCK)
            value = jnp.dot(turned[:, cols], parity_v[...], preferred_element_type=f32).astype(bf16)
            half = pl.ds(pl.multiple_of(b * LANES, LANES), LANES)
            for parity in range(2):
                sorted_v[parity, :, half] = value[:, parity * LANES : (parity + 1) * LANES]
            return carry

        lax.fori_loop(0, depth // BLOCK, sort, 0)
        four_loads[q].wait()
        if q == count - 1:
            grads_load.wait()

        def synthesise(start, width):
            cols = pl.ds(start, width)
            rows = slice(groups * at // 2, groups * (at + size) // 2)
            values = []
            for parity in range(2):
                value = jnp.dot(
                    sorted_v[parity, :, 0 : depth // 2], four_v[parity, rows, cols], preferred_element_type=f32
                )
                values.append(value if q == 0 else value + phys[parity, :, cols])
            if q < count - 1:
                for parity in range(2):
                    phys[parity, :, cols] = values[parity]
                return
            forces = []
            for half in range(2):
                value = values[0] + values[1] if half == 0 else values[0] - values[1]
                first, second = value[0:SHARE], value[LANES : LANES + SHARE]
                g = [grads_v[i, 0, :, pl.ds(start + half * half_z, width)].astype(f32) for i in range(4)]
                forces.append((g[0] * first + g[2] * second, g[1] * first + g[3] * second))
            for c in range(2):
                rows = slice(c * LANES, c * LANES + SHARE)
                force[0, rows, cols] = (forces[0][c] + forces[1][c]).astype(bf16)
                force[1, rows, cols] = (forces[0][c] - forces[1][c]).astype(bf16)

        def synthesise_one(n, carry):
            synthesise(pl.multiple_of(n * WIDTH, LANES), WIDTH)
            return carry

        lax.fori_loop(0, half_z // WIDTH, synthesise_one, 0)
        if half_z % WIDTH:
            synthesise(half_z // WIDTH * WIDTH, half_z % WIDTH)

    def analyse(q):
        size, at = chunks[q], starts[q]
        several = BLOCK // size

        def one(n, carry):
            rows = pl.ds(pl.multiple_of(groups * at // 2 + n * BLOCK, BLOCK), BLOCK)
            halves = [
                lax.dot_general(four_v[parity, rows, :], force[parity], NT, preferred_element_type=f32).astype(bf16)
                for parity in range(2)
            ]
            for b in range(2):
                part = slice(b * LANES, (b + 1) * LANES)
                value = jnp.concatenate([halves[0][part], halves[1][part]], axis=0)
                value = jnp.dot(parity_v[...], value, preferred_element_type=f32).astype(bf16)
                for j in range(several):
                    block = value[j * size : (j + 1) * size]
                    letter = pack(block[:, :LANES], block[:, LANES:])
                    send_c[(2 * n + b) * several + j, packed(q)] = letter
            return carry

        lax.fori_loop(0, groups // (2 * several), one, 0)
        exchange("col", 2, q, send_c, recv_c)

    def update(q):
        size, at = chunks[q], starts[q]
        arrived(2, q, recv_c)
        gather(q, recv_c)

        def one(n, carry):
            cols = pl.ds(pl.multiple_of(n * (384 * quads), 384), 384 * quads)
            value = jnp.dot(lhs[0 : 2 * size, :], cheb_v[:, cols], preferred_element_type=f32)
            value = solved[2 * at : 2 * (at + size), cols] + f32(step_weight) * value
            post(n, q, value.astype(bf16), send_d)
            return carry

        lax.fori_loop(0, groups // (4 * quads), one, 0)
        exchange("row", 3, q, send_d, recv_d)

    def finish(q):
        size, at = chunks[q], starts[q]
        arrived(3, q, recv_d)

        def one(s, carry):
            some = pl.ds(s * BATCH, BATCH)
            for c, part in enumerate(unpack(recv_d[some, packed(q)])):
                out_v[c, some, pl.ds(at, size), :] = part[..., :SHARE]
            return carry

        lax.fori_loop(0, groups // BATCH, one, 0)
        return local(out_v.at[:, :, pl.ds(at, size)], out.at[:, :, pl.ds(at, size)], out_sem.at[q])

    for q in range(count):
        to_points(q)
    for q in range(count):
        to_physical(q)
    order = list(reversed(range(count)))
    for q in order:
        analyse(q)
    for q in order:
        update(q)
    writes = [finish(q) for q in order]
    for q in range(count):
        for phase, send in enumerate((send_a, send_b, send_c, send_d)):
            sent(phase, q, send)
        writes[q].wait()


def on_device(groups, chunks, adjoint_in, solve_inverse, gradient_fields):
    local_modes = adjoint_in.shape[2]
    length_y = solve_inverse.shape[1]
    points_z = gradient_fields.shape[3]
    cheb = jnp.asarray(cheb_build(length_y))
    parity = jnp.asarray(parity_build())
    four = jnp.asarray(fourier_build(local_modes * groups, points_z, groups, chunks))
    f32, bf16 = jnp.float32, jnp.bfloat16
    most = max(chunks)
    count = len(chunks)
    mail = pltpu.VMEM((groups, local_modes * 3 // 2, LANES), bf16)
    result = pl.pallas_call(
        functools.partial(kernel, chunks),
        out_shape=jax.ShapeDtypeStruct(adjoint_in.shape, bf16),
        in_specs=[pl.BlockSpec(memory_space=pl.ANY)] * 6,
        out_specs=pl.BlockSpec(memory_space=pl.ANY),
        scratch_shapes=[
            pltpu.VMEM(adjoint_in.shape, bf16),
            pltpu.VMEM(solve_inverse.shape[1:], bf16),
            pltpu.VMEM(gradient_fields.shape, bf16),
            pltpu.VMEM(cheb.shape, bf16),
            pltpu.VMEM(four.shape, bf16),
            pltpu.VMEM(parity.shape, bf16),
            *[mail] * 8,
            pltpu.VMEM((2 * most, length_y), bf16),
            pltpu.VMEM((2 * local_modes, length_y), f32),
            pltpu.VMEM((2 * most, length_y), bf16),
            pltpu.VMEM((2 * LANES, groups * most), bf16),
            pltpu.VMEM((2, 2 * LANES, groups * most // 2), bf16),
            pltpu.VMEM((2, 2 * LANES, points_z // 2), f32),
            pltpu.VMEM((2, 2 * LANES, points_z // 2), bf16),
            pltpu.VMEM(adjoint_in.shape, bf16),
            pltpu.SemaphoreType.DMA((2 * count + 4,)),
            pltpu.SemaphoreType.DMA((4, count)),
            pltpu.SemaphoreType.DMA((4, count)),
            pltpu.SemaphoreType.DMA((count,)),
        ],
        compiler_params=pltpu.CompilerParams(
            collective_id=0, has_side_effects=True, vmem_limit_bytes=VMEM_LIMIT
        ),
        cost_estimate=pl.CostEstimate(flops=12_000_000_000, bytes_accessed=40_000_000, transcendentals=0),
    )(adjoint_in, solve_inverse, gradient_fields, cheb, four, parity)
    return result.astype(f32)


def solution(mesh):
    groups = mesh.shape["row"]
    return jax.shard_map(
        functools.partial(on_device, groups, CHUNKS),
        mesh=mesh,
        in_specs=(P(None, None, "col", "row"), P("row", None, None), P(None, "row", "col", None)),
        out_specs=P(None, None, "col", "row"),
        check_vma=False,
    )
```

```python
import functools
import math

import jax
import jax.numpy as jnp
import ml_dtypes
import numpy as np
from jax import lax
from jax.experimental import pallas as pl
from jax.experimental.pallas import tpu as pltpu
from jax.sharding import PartitionSpec as P

NY = 1536
NZ = 3840
KZ = 2560

step_weight = 0.5

LANES = 128
BLOCK = 256
BATCH = 16
SHARE = 96
CHUNKS = (64, 32, 32, 32)
SOLVE_TILE = 768
POST = 4
WIDTH = 640
VMEM_LIMIT = 60 * 1024 * 1024
MESH = pl.DeviceIdType.MESH
NT = (((1,), (1,)), ((), ()))


def cheb_build(length_y):
    index = np.arange(length_y, dtype=np.int64)
    residue = index[:, None] * index[None, :] % (2 * (length_y - 1))
    table = np.cos(np.arange(2 * (length_y - 1)) * (math.pi / (length_y - 1))) * math.sqrt(2.0 / length_y)
    return table.astype(np.float32).astype(ml_dtypes.bfloat16)[residue]


def parity_order():
    n = np.arange(BLOCK)
    odd = (n + 1) // 2 % 2
    return np.concatenate([n[odd == 0], n[odd == 1]])


def parity_build():
    forward = np.zeros((BLOCK, BLOCK), np.float32)
    forward[parity_order(), np.arange(BLOCK)] = 1.0
    return forward.astype(ml_dtypes.bfloat16)


def fourier_build(modes, points_z, devices, chunks):
    local = np.arange(modes, dtype=np.int64).reshape(devices, modes // devices)
    starts = np.cumsum((0,) + chunks)
    k = np.concatenate([local[:, a:b].reshape(-1) for a, b in zip(starts[:-1], starts[1:])])
    k = k.reshape(-1, BLOCK)[:, parity_order()].reshape(-1, 2, BLOCK // 2)
    k = k.transpose(1, 0, 2).reshape(2, modes // 2, 1)
    residue = (k + 1) // 2 * np.arange(points_z // 2, dtype=np.int64) % points_z
    angles = np.arange(points_z) * (2.0 * math.pi / points_z)
    both = np.stack([np.cos(angles), np.sin(angles)]) * math.sqrt(2.0 / points_z)
    both = both.astype(np.float32).astype(ml_dtypes.bfloat16)
    return both[k % 2, residue]


def below(shape, limit):
    return lax.broadcasted_iota(jnp.int16, shape, len(shape) - 1) < jnp.int16(limit)


def pack(first, second):
    half, last = first.shape[-2] // 2, first.ndim - 1
    turned = pltpu.roll(second, 96, last)
    top = jnp.where(below(first.shape, 96), first, turned)
    upper, lower = turned[..., :half, :], turned[..., half:, :]
    low = jnp.where(below(upper.shape, 64), upper, pltpu.roll(lower, 64, last))
    return jnp.concatenate([top, low], axis=last - 1)


def unpack(block):
    rows, last = block.shape[-2] * 2 // 3, block.ndim - 1
    top, low = block[..., :rows, :], block[..., rows:, :]
    full = jnp.concatenate([low, pltpu.roll(low, 64, last)], axis=last - 1)
    second = pltpu.roll(jnp.where(below(top.shape, 64), full, top), 32, last)
    return top, second


def spread_lanes(tiles):
    shape = tiles[0].shape
    middle = [pltpu.roll(t, 32, 1) for t in tiles[:2]], [pltpu.roll(t, 64, 1) for t in tiles[1:]]
    return [
        tiles[0],
        jnp.where(below(shape, 32), *middle[0]),
        jnp.where(below(shape, 64), *middle[1]),
        pltpu.roll(tiles[2], 96, 1),
    ]


def close_lanes(parts):
    shape = parts[0].shape
    turned = [pltpu.roll(p, shift, 1) for p, shift in zip(parts[1:], (96, 64, 32))]
    return [
        jnp.where(below(shape, 96), parts[0], turned[0]),
        jnp.where(below(shape, 64), turned[0], turned[1]),
        jnp.where(below(shape, 32), turned[1], turned[2]),
    ]


def kernel(
    chunks, adj, inv, grads, cheb, four, parity, out,
    adj_v, inv_v, grads_v, cheb_v, four_v, parity_v,
    send_a, recv_a, send_b, recv_b, send_c, recv_c, send_d, recv_d,
    lhs, solved, rounded, turned, sorted_v, phys, force, out_v,
    load_sem, send_sem, recv_sem, out_sem,
):
    f32, bf16 = jnp.float32, jnp.bfloat16
    groups = adj.shape[1]
    length_y = inv.shape[1]
    half_z = four.shape[2]
    row, col = lax.axis_index("row"), lax.axis_index("col")
    starts = [sum(chunks[:q]) for q in range(len(chunks))]
    count = len(chunks)
    tile = math.gcd(length_y, SOLVE_TILE)
    quads = min(POST, groups // 4)

    def local(source, target, sem):
        copy = pltpu.make_async_copy(source, target, sem)
        copy.start()
        return copy

    adj_loads = [
        local(adj.at[:, :, pl.ds(starts[q], chunks[q])], adj_v.at[:, :, pl.ds(starts[q], chunks[q])], load_sem.at[q])
        for q in range(count)
    ]
    barrier = pltpu.get_barrier_semaphore()

    def greet(t, carry):
        pl.semaphore_signal(barrier, inc=1, device_id={"row": lax.rem(row + t, groups)}, device_id_type=MESH)
        pl.semaphore_signal(barrier, inc=1, device_id={"col": lax.rem(col + t, groups)}, device_id_type=MESH)
        return carry

    lax.fori_loop(1, groups, greet, 0)
    def packed(q):
        return pl.ds(starts[q] * 3 // 2, chunks[q] * 3 // 2)

    def exchange_one(axis, phase, q, t, send, recv):
        me = row if axis == "row" else col
        peer = lax.rem(me + t, groups)
        pltpu.make_async_remote_copy(
            src_ref=send.at[peer, packed(q)],
            dst_ref=recv.at[me, packed(q)],
            send_sem=send_sem.at[phase, q],
            recv_sem=recv_sem.at[phase, q],
            device_id={axis: peer},
            device_id_type=MESH,
        ).start()

    def exchange(axis, phase, q, send, recv):
        def one(t, carry):
            exchange_one(axis, phase, q, t, send, recv)
            return carry

        lax.fori_loop(1, groups, one, 0)
        me = row if axis == "row" else col
        recv[me, packed(q)] = send[me, packed(q)]

    def arrived(phase, q, recv):
        every = recv.at[pl.ds(0, groups - 1), packed(q)]
        pltpu.make_async_copy(every, every, recv_sem.at[phase, q]).wait()

    def sent(phase, q, send):
        every = send.at[pl.ds(0, groups - 1), packed(q)]
        pltpu.make_async_copy(every, every, send_sem.at[phase, q]).wait()

    def clear(t, carry):
        for half in range(2):
            for c in range(2):
                force[half, c * LANES + SHARE : (c + 1) * LANES, :] = jnp.zeros((LANES - SHARE, half_z), bf16)
        return carry

    for q in range(count):
        size, at = chunks[q], starts[q]
        adj_loads[q].wait()

        def spread(p, carry, size=size, at=at, q=q):
            blank = jnp.zeros((BATCH, size, LANES - SHARE), bf16)
            some = pl.ds(p * BATCH, BATCH)
            parts = [jnp.concatenate([adj_v[c, some, pl.ds(at, size), :], blank], axis=2) for c in range(2)]
            send_a[some, packed(q)] = pack(*parts)
            return carry

        lax.fori_loop(0, groups // BATCH, spread, 0)
        if q == 0:
            lax.fori_loop(0, 1, clear, 0)
            pl.semaphore_wait(barrier, 2 * (groups - 1))
        exchange("row", 0, q, send_a, recv_a)

    inv_load = local(inv.at[0], inv_v, load_sem.at[count])
    cheb_load = local(cheb, cheb_v, load_sem.at[count + 1])
    parity_load = local(parity, parity_v, load_sem.at[count + 3])
    four_loads = []
    for q in range(count):
        part = pl.ds(groups * starts[q] // 2, groups * chunks[q] // 2)
        four_loads.append(local(four.at[:, part], four_v.at[:, part], load_sem.at[count + 4 + q]))
    grads_load = local(grads, grads_v, load_sem.at[count + 2])

    def gather(q, recv):
        size = chunks[q]

        def one(s, carry):
            first, second = unpack(recv[pl.ds(s * BATCH, BATCH), packed(q)])
            for c, parts in enumerate((first, second)):
                for quad in range(BATCH // 4):
                    for i, tile in enumerate(close_lanes([parts[4 * quad + i] for i in range(4)])):
                        at = pl.ds(pl.multiple_of(s * (BATCH * SHARE), LANES) + (3 * quad + i) * LANES, LANES)
                        lhs[c * size : (c + 1) * size, at] = tile
            return carry

        lax.fori_loop(0, groups // BATCH, one, 0)

    def post(n, q, value, send):
        size = chunks[q]
        for quad in range(quads):
            tiles = [slice((3 * quad + i) * LANES, (3 * quad + i + 1) * LANES) for i in range(3)]
            first, second = (
                spread_lanes([value[c * size : (c + 1) * size, tile] for tile in tiles]) for c in range(2)
            )
            for j in range(4):
                send[4 * (quads * n + quad) + j, packed(q)] = pack(first[j], second[j])

    def to_points(q):
        size, at = chunks[q], starts[q]
        arrived(0, q, recv_a)
        gather(q, recv_a)
        if q == 0:
            inv_load.wait()

        def solve(n, carry):
            cols = pl.ds(pl.multiple_of(n * tile, tile), tile)
            value = jnp.dot(lhs[0 : 2 * size, :], inv_v[:, cols], preferred_element_type=f32)
            solved[2 * at : 2 * (at + size), cols] = value
            rounded[0 : 2 * size, cols] = value.astype(bf16)
            return carry

        lax.fori_loop(0, length_y // tile, solve, 0)
        if q == 0:
            cheb_load.wait()

        def evaluate(n, carry):
            cols = pl.ds(pl.multiple_of(n * (384 * quads), 384), 384 * quads)
            value = jnp.dot(rounded[0 : 2 * size, :], cheb_v[:, cols], preferred_element_type=f32)
            post(n, q, value.astype(bf16), send_b)
            return carry

        lax.fori_loop(0, groups // (4 * quads), evaluate, 0)
        exchange("col", 1, q, send_b, recv_b)

    def to_physical(q):
        size, at = chunks[q], starts[q]
        depth = groups * size
        arrived(1, q, recv_b)

        def one(s, carry):
            rows = pl.ds(pl.multiple_of(s * (BATCH * size), LANES), BATCH * size)
            for c, part in enumerate(unpack(recv_b[pl.ds(s * BATCH, BATCH), packed(q)])):
                turned[c * LANES : (c + 1) * LANES, rows] = part.reshape(BATCH * size, LANES).T
            return carry

        lax.fori_loop(0, groups // BATCH, one, 0)
        if q == 0:
            parity_load.wait()

        def sort(b, carry):
            cols = pl.ds(pl.multiple_of(b * BLOCK, BLOCK), BLOCK)
            value = jnp.dot(turned[:, cols], parity_v[...], preferred_element_type=f32).astype(bf16)
            half = pl.ds(pl.multiple_of(b * LANES, LANES), LANES)
            for parity in range(2):
                sorted_v[parity, :, half] = value[:, parity * LANES : (parity + 1) * LANES]
            return carry

        lax.fori_loop(0, depth // BLOCK, sort, 0)
        four_loads[q].wait()
        if q == count - 1:
            grads_load.wait()

        def synthesise(start, width):
            cols = pl.ds(start, width)
            rows = slice(groups * at // 2, groups * (at + size) // 2)
            values = []
            for parity in range(2):
                value = jnp.dot(
                    sorted_v[parity, :, 0 : depth // 2], four_v[parity, rows, cols], preferred_element_type=f32
                )
                values.append(value if q == 0 else value + phys[parity, :, cols])
            if q < count - 1:
                for parity in range(2):
                    phys[parity, :, cols] = values[parity]
                return
            forces = []
            for half in range(2):
                value = values[0] + values[1] if half == 0 else values[0] - values[1]
                first, second = value[0:SHARE], value[LANES : LANES + SHARE]
                g = [grads_v[i, 0, :, pl.ds(start + half * half_z, width)].astype(f32) for i in range(4)]
                forces.append((g[0] * first + g[2] * second, g[1] * first + g[3] * second))
            for c in range(2):
                rows = slice(c * LANES, c * LANES + SHARE)
                force[0, rows, cols] = (forces[0][c] + forces[1][c]).astype(bf16)
                force[1, rows, cols] = (forces[0][c] - forces[1][c]).astype(bf16)

        def synthesise_one(n, carry):
            synthesise(pl.multiple_of(n * WIDTH, LANES), WIDTH)
            return carry

        lax.fori_loop(0, half_z // WIDTH, synthesise_one, 0)
        if half_z % WIDTH:
            synthesise(half_z // WIDTH * WIDTH, half_z % WIDTH)

    def analyse(q):
        size, at = chunks[q], starts[q]
        several = BLOCK // size

        def one(n, carry):
            rows = pl.ds(pl.multiple_of(groups * at // 2 + n * BLOCK, BLOCK), BLOCK)
            halves = [
                lax.dot_general(four_v[parity, rows, :], force[parity], NT, preferred_element_type=f32).astype(bf16)
                for parity in range(2)
            ]
            for b in range(2):
                part = slice(b * LANES, (b + 1) * LANES)
                value = jnp.concatenate([halves[0][part], halves[1][part]], axis=0)
                value = jnp.dot(parity_v[...], value, preferred_element_type=f32).astype(bf16)
                for j in range(several):
                    block = value[j * size : (j + 1) * size]
                    letter = pack(block[:, :LANES], block[:, LANES:])
                    send_c[(2 * n + b) * several + j, packed(q)] = letter
            return carry

        lax.fori_loop(0, groups // (2 * several), one, 0)
        exchange("col", 2, q, send_c, recv_c)

    def update(q):
        size, at = chunks[q], starts[q]
        arrived(2, q, recv_c)
        gather(q, recv_c)

        def one(n, carry):
            cols = pl.ds(pl.multiple_of(n * (384 * quads), 384), 384 * quads)
            value = jnp.dot(lhs[0 : 2 * size, :], cheb_v[:, cols], preferred_element_type=f32)
            value = solved[2 * at : 2 * (at + size), cols] + f32(step_weight) * value
            post(n, q, value.astype(bf16), send_d)
            return carry

        lax.fori_loop(0, groups // (4 * quads), one, 0)
        exchange("row", 3, q, send_d, recv_d)

    def finish(q):
        size, at = chunks[q], starts[q]
        arrived(3, q, recv_d)

        def one(s, carry):
            some = pl.ds(s * BATCH, BATCH)
            for c, part in enumerate(unpack(recv_d[some, packed(q)])):
                out_v[c, some, pl.ds(at, size), :] = part[..., :SHARE]
            return carry

        lax.fori_loop(0, groups // BATCH, one, 0)
        return local(out_v.at[:, :, pl.ds(at, size)], out.at[:, :, pl.ds(at, size)], out_sem.at[q])

    for q in range(count):
        to_points(q)
    for q in range(count):
        to_physical(q)
    order = list(reversed(range(count)))
    for q in order:
        analyse(q)
    for q in order:
        update(q)
    writes = [finish(q) for q in order]
    for q in range(count):
        for phase, send in enumerate((send_a, send_b, send_c, send_d)):
            sent(phase, q, send)
        writes[q].wait()


def on_device(groups, chunks, adjoint_in, solve_inverse, gradient_fields):
    local_modes = adjoint_in.shape[2]
    length_y = solve_inverse.shape[1]
    points_z = gradient_fields.shape[3]
    cheb = jnp.asarray(cheb_build(length_y))
    parity = jnp.asarray(parity_build())
    four = jnp.asarray(fourier_build(local_modes * groups, points_z, groups, chunks))
    f32, bf16 = jnp.float32, jnp.bfloat16
    most = max(chunks)
    count = len(chunks)
    mail = pltpu.VMEM((groups, local_modes * 3 // 2, LANES), bf16)
    result = pl.pallas_call(
        functools.partial(kernel, chunks),
        out_shape=jax.ShapeDtypeStruct(adjoint_in.shape, bf16),
        in_specs=[pl.BlockSpec(memory_space=pl.ANY)] * 6,
        out_specs=pl.BlockSpec(memory_space=pl.ANY),
        scratch_shapes=[
            pltpu.VMEM(adjoint_in.shape, bf16),
            pltpu.VMEM(solve_inverse.shape[1:], bf16),
            pltpu.VMEM(gradient_fields.shape, bf16),
            pltpu.VMEM(cheb.shape, bf16),
            pltpu.VMEM(four.shape, bf16),
            pltpu.VMEM(parity.shape, bf16),
            *[mail] * 8,
            pltpu.VMEM((2 * most, length_y), bf16),
            pltpu.VMEM((2 * local_modes, length_y), f32),
            pltpu.VMEM((2 * most, length_y), bf16),
            pltpu.VMEM((2 * LANES, groups * most), bf16),
            pltpu.VMEM((2, 2 * LANES, groups * most // 2), bf16),
            pltpu.VMEM((2, 2 * LANES, points_z // 2), f32),
            pltpu.VMEM((2, 2 * LANES, points_z // 2), bf16),
            pltpu.VMEM(adjoint_in.shape, bf16),
            pltpu.SemaphoreType.DMA((2 * count + 4,)),
            pltpu.SemaphoreType.DMA((4, count)),
            pltpu.SemaphoreType.DMA((4, count)),
            pltpu.SemaphoreType.DMA((count,)),
        ],
        compiler_params=pltpu.CompilerParams(
            collective_id=0, has_side_effects=True, vmem_limit_bytes=VMEM_LIMIT
        ),
        cost_estimate=pl.CostEstimate(flops=12_000_000_000, bytes_accessed=40_000_000, transcendentals=0),
    )(adjoint_in, solve_inverse, gradient_fields, cheb, four, parity)
    return result.astype(f32)


def solution(mesh):
    groups = mesh.shape["row"]
    return jax.shard_map(
        functools.partial(on_device, groups, CHUNKS),
        mesh=mesh,
        in_specs=(P(None, None, "col", "row"), P("row", None, None), P(None, "row", "col", None)),
        out_specs=P(None, None, "col", "row"),
        check_vma=False,
    )
```
